128 devices in a mesh: rep: 32 (over x, z, core), tp: 4 (over y).
Axes of the slice: x: 4, y: 4, z: 4, core: 2. Of those that a mesh axis runs over, the one named last changes fastest.
Arguments:
- hidden_in: bfloat16 [49152, 5120], P('rep', 'tp'), may hold values from -6 to 6
- ln_gain: float32 [5120], replicated, may hold values from 0.5 to 1.5
- w_query: bfloat16 [5120, 4096], P(None, 'tp'), may hold values from -0.078125 to 0.078125
- key_value_weight: bfloat16 [5120, 4, 256], P(None, 'tp'), may hold values from -0.078125 to 0.078125
- q_gain: float32 [128], replicated, may hold values from 0.25 to 1.75
- k_gain: float32 [128], replicated, may hold values from 0.25 to 1.75
- key_value_cache: bfloat16 [2048, 64, 4, 256], P('rep', None, 'tp'), may hold values from -256 to 256
- prefix_pages: int32 [32, 4], replicated, may hold values from 1 to 16, as said below
- page_holder: int32 [32, 4, 16], replicated, may hold values from 0 to 31, as said below
- page_slot: int32 [32, 4, 16], replicated, may hold values from 0 to 63
- span_pages: int32 [32, 4], replicated, may hold values from 1 to 12, 24 in all within a row
- decode_target: int32 [32, 24, 1], replicated, may hold values from 0 to 31; in each aligned block of 24 rows (0 to 23, 24 to 47, ..., all dimensions but the last counted through in order) at most 2 rows name the same one
Outputs:
- attn_out: bfloat16 [49152, 4096], P('rep', 'tp')
- pushed: bfloat16 [2048, 64, 4, 256], P('rep', None, 'tp')
The draws below stay inside these ranges and needn't reach their ends.
Inputs may be any that keep to these rules, and one draw needn't show every extreme that they name: `prefix_pages`: in every draw some replica has all its sessions at 16 pages. `page_holder`: of the 64 page positions of one replica's sessions, used or not, exactly 2 name each holder. `span_pages`: each replica's row sums to 24 and its largest entry is 12. `decode_target`: among the 24 pages of one replica no decode replica is named more than 2 times, and in some replica one is named exactly 2 times.
All inputs are finite; a program needn't handle non-finite values.
Results may differ from the reference program's by a relative error of at most 0.0045.
The reference program's roundings to bfloat16 on the way count: a program that leaves them out, or rounds other values in their place, can miss the bound.
Values may be sent and summed in bfloat16 or wider, within the bound.
No kernel may reach another device: no remote copies, remote signals or barrier semaphores. Data moves between devices by JAX's collectives and lax.ppermute only.
A program may use at most 192 MiB of HBM per device.

```python
import math
import jax
import jax.numpy as jnp
import numpy as np
from jax import lax

MODEL_WIDTH = 5120
HQ = 32
KEY_VALUE_HEADS = 4
HEAD_SIZE = 128
PAGE_TOKENS = 64
REPLICA_SESSIONS = 4
SPAN_PAGES_REP = 24
PREFIX_PAGE_MAX = 16
PAGES_DEV = 64
MOSTC = 12
CAP = 2
PUSHCAP = 2
SPAN_TOKEN_TOTAL = 49152
CACHE_PAGE_TOTAL = 2048
NPUSH = 2048
N_REP = 32


def draw_key_value_cache(key, part):
    key = jax.random.fold_in(key, 13)
    base_key = jax.random.fold_in(key, 0)
    array_shape = (CACHE_PAGE_TOTAL, PAGE_TOKENS, KEY_VALUE_HEADS, 2 * HEAD_SIZE)
    base = jnp.clip(jax.random.normal(base_key, array_shape, jnp.float32), -6.0, 6.0)
    return base.astype(jnp.bfloat16)


def draw_prefix_pages(key, part):
    key = jax.random.fold_in(key, 7)
    length_key, full_key = jax.random.split(key)
    lengths = jax.random.randint(length_key, (N_REP, REPLICA_SESSIONS), 1, PREFIX_PAGE_MAX + 1)
    full_row = jax.random.randint(full_key, (), 0, N_REP)
    rows = jnp.arange(N_REP, dtype=jnp.int32)[:, None]
    return jnp.where(rows == full_row, PREFIX_PAGE_MAX, lengths).astype(jnp.int32)


def draw_page_holder(key, part):
    key = jax.random.fold_in(key, 5)
    perm_key, order_key = jax.random.split(key)
    holders = jax.vmap(lambda single: jax.random.permutation(single, N_REP))(jax.random.split(perm_key, N_REP))
    orders = jax.vmap(lambda single: jax.random.permutation(single, REPLICA_SESSIONS * PREFIX_PAGE_MAX))(jax.random.split(order_key, N_REP))
    chosen = jnp.take_along_axis(holders, orders // CAP, axis=1)
    return chosen.reshape(N_REP, REPLICA_SESSIONS, PREFIX_PAGE_MAX).astype(jnp.int32)


def plant(entries, rng, smallest, high):
    index_at = [jax.random.randint(jax.random.fold_in(rng, axis), (), 0, length) for axis, length in enumerate(entries.shape)]
    longest = entries.shape.index(max(entries.shape))
    neighbour = index_at[:longest] + [(index_at[longest] + 1) % entries.shape[longest]] + index_at[longest + 1:]
    return entries.at[tuple(index_at)].set(smallest).at[tuple(neighbour)].set(high)


def levels(key, shape, cuts, smallest, largest):
    def one(axis_at, parts):
        steps = jax.random.uniform(jax.random.fold_in(jax.random.fold_in(key, 6), axis_at), (parts,), jnp.float32, smallest / len(cuts), largest / len(cuts))
        return jnp.repeat(jnp.exp(steps), shape[axis_at] // parts).reshape((-1,) + (1,) * (len(shape) - axis_at - 1))

    level = one(*cuts[0])
    for cut in cuts[1:]:
        level = level * one(*cut)
    return level


def split_up(count, total, bound, lean):
    loads = [(1 << 20) // math.isqrt(rank ** lean) + 1 for rank in range(2, count + 1)]
    rest, given = total - bound - (count - 1), [1] * (count - 1)
    while rest > 0:
        candidates = [i for i in range(count - 1) if given[i] < bound]
        whole, budget = sum([loads[i] for i in candidates]), rest
        for i in candidates:
            extra = min(bound - given[i], max(1, budget * loads[i] // whole), rest)
            given[i] = given[i] + extra
            rest = rest - extra
    return np.array([bound] + given)


def uneven(own_key, amount, total, most, lean):
    if amount == 2:
        one = jax.random.randint(own_key, (), max(1, total - most), min(most, total - 1) + 1)
        return jnp.stack([one, total - one])
    tallies = jnp.asarray(split_up(amount, total, most, lean), jnp.int32)
    couples = (amount - 1) // 2
    giver, taker = tallies[1:1 + 2 * couples:2], tallies[2:2 + 2 * couples:2]
    room = jnp.minimum(giver - 1, most - taker)
    moved = jax.random.randint(jax.random.fold_in(own_key, 1), (couples,), 0, 1 << 20) % (room + 1)
    tallies = tallies.at[1:1 + 2 * couples:2].set(giver - moved).at[2:2 + 2 * couples:2].set(taker + moved)
    return tallies[jax.random.permutation(jax.random.fold_in(own_key, 2), amount)]


def assign_block(own_key, own, number, rows, number_of, top, limit, lean):
    sequence = jax.random.permutation(own_key, number_of)
    crowded, common = load_shares(number_of, rows * top, limit, lean, True), load_shares(number_of, rows * top, limit, lean, False)
    places = jnp.arange(number_of)

    def named(tallies, turn):
        used = int((tallies > 0).sum())
        fixed = max(1, used // 4)
        moved = fixed + (places - fixed + turn * (used - fixed)) % max(1, number_of - fixed)
        return jnp.zeros((number_of,), jnp.int32).at[sequence[jnp.where(places < fixed, places, moved)]].set(jnp.asarray(tallies, jnp.int32))

    tallies = jnp.where(number % 4 == 0, named(crowded, number // 4), named(common, number - number // 4 - 1))
    mixed = jax.random.permutation(jax.random.fold_in(own, 3), number_of)
    giver, taker = mixed[0:number_of // 2 * 2:2], mixed[1:number_of // 2 * 2:2]
    room = jnp.minimum(tallies[giver] - 1, limit - tallies[taker]) // 2
    room = jnp.where((giver == sequence[0]) | (taker == sequence[0]) | (tallies[taker] == 0), 0, jnp.maximum(room, 0))
    moved = jax.random.randint(jax.random.fold_in(own, 4), (number_of // 2,), 0, 1 << 20) % (room + 1)
    tallies = tallies.at[giver].add(-moved).at[taker].add(moved)
    items = jnp.searchsorted(jnp.cumsum(tallies), jnp.arange(rows * top), side="right").astype(jnp.int32)
    listing = items.reshape(top, rows).T
    listing = listing[jax.random.permutation(jax.random.fold_in(own, 1), rows)]
    turn = jax.random.randint(jax.random.fold_in(own, 2), (rows, 1), 0, top)
    return jnp.take_along_axis(listing, (jnp.arange(top)[None, :] + turn) % top, axis=1)


def load_shares(amount, total, bound, slope, full):
    weights = [(1 << 20) // math.isqrt(rank ** slope) + 1 for rank in range(1, amount + 1)]
    largest = bound if full else min(bound, max(-(-total // amount), total * weights[0] // sum(weights)))
    least = 1 if total - largest >= amount - 1 else 0
    given, rest = [largest] + [least] * (amount - 1), total - largest - least * (amount - 1)
    while rest > 0:
        candidates = [i for i in range(1, amount) if given[i] < largest] or [i for i in range(1, amount) if given[i] < bound]
        pool, left = sum([weights[i] for i in candidates]), rest
        for i in candidates:
            extra = min(bound - given[i], max(1, left * weights[i] // pool), rest)
            given[i] = given[i] + extra
            rest = rest - extra
    return np.array(given)


def centred(own_key, shape, scale, bound, cuts=(), kind=jnp.bfloat16):
    level = levels(own_key, shape, cuts, -0.22, 0.18) if cuts else 1.0
    array = jax.random.normal(own_key, shape, jnp.float32) * scale * level
    return jnp.minimum(jnp.maximum(array, -bound), bound).astype(kind)


def setup_inputs(seed: int = 0) -> dict:
    keys = jax.random.split(jax.random.key(seed), 13)
    hidden_in = centred(keys[0], (SPAN_TOKEN_TOTAL, MODEL_WIDTH), 1.0, 6.0, ((0, 32), (1, 4)))
    ln_gain = jnp.clip(1.0 + 0.1 * jax.random.normal(keys[1], (MODEL_WIDTH,), jnp.float32), 0.5, 1.5)
    w_query = centred(keys[2], (MODEL_WIDTH, HQ * HEAD_SIZE), MODEL_WIDTH ** -0.5, 0.078125, ((1, 4),))
    key_value_weight = centred(keys[3], (MODEL_WIDTH, KEY_VALUE_HEADS, 2 * HEAD_SIZE), MODEL_WIDTH ** -0.5, 0.078125, ((1, 4),))
    q_gain = jnp.clip(1.0 + 0.15 * jax.random.normal(keys[4], (HEAD_SIZE,), jnp.float32), 0.25, 1.75)
    k_gain = jnp.clip(1.0 + 0.15 * jax.random.normal(keys[5], (HEAD_SIZE,), jnp.float32), 0.25, 1.75)
    key_value_cache = draw_key_value_cache(jax.random.fold_in(keys[12], 71), 0)
    prefix_pages = draw_prefix_pages(jax.random.fold_in(keys[12], 71), 0)
    page_holder = draw_page_holder(jax.random.fold_in(keys[12], 71), 0)
    page_slot = plant(jax.random.randint(keys[9], (N_REP, REPLICA_SESSIONS, PREFIX_PAGE_MAX), 0, PAGES_DEV), jax.random.fold_in(keys[9], 1), 0, PAGES_DEV - 1).astype(jnp.int32)
    span_pages = jax.vmap(lambda own: uneven(own, REPLICA_SESSIONS, SPAN_PAGES_REP, MOSTC, 1))(jax.random.split(keys[10], N_REP)).reshape((N_REP, REPLICA_SESSIONS)).astype(jnp.int32)
    decode_target_keys = jax.random.split(jax.random.fold_in(keys[11], 1), N_REP * SPAN_PAGES_REP // SPAN_PAGES_REP)
    decode_target_turns = jax.random.permutation(jax.random.fold_in(keys[11], 3), N_REP * SPAN_PAGES_REP // SPAN_PAGES_REP)
    decode_target = jax.vmap(lambda own, number: assign_block(jax.random.fold_in(keys[11], 2), own, number, SPAN_PAGES_REP, N_REP, 1, PUSHCAP, 1))(decode_target_keys, decode_target_turns).reshape((N_REP, SPAN_PAGES_REP, 1))
    return {"hidden_in": hidden_in, "ln_gain": ln_gain, "w_query": w_query, "key_value_weight": key_value_weight, "q_gain": q_gain, "k_gain": k_gain, "key_value_cache": key_value_cache, "prefix_pages": prefix_pages, "page_holder": page_holder, "page_slot": page_slot, "span_pages": span_pages, "decode_target": decode_target}


def rms_scale(values, gain):
    mean_square = lax.optimization_barrier(jnp.mean(values * values, axis=-1, keepdims=True))
    return values * lax.rsqrt(mean_square + 1e-06) * gain

def rotary(values, positions):
    half_dim = values.shape[-1] // 2
    exponent = jnp.arange(half_dim, dtype=jnp.float32) * (2.0 / values.shape[-1])
    inverse = jnp.power(jnp.float32(1000000.0), -exponent)
    angles = positions.astype(jnp.float32)[:, None] * inverse[None, :]
    cosine = jnp.concatenate([jnp.cos(angles), jnp.cos(angles)], -1)[:, None, :]
    sine = jnp.concatenate([jnp.sin(angles), jnp.sin(angles)], -1)[:, None, :]
    rotated = jnp.concatenate([-values[..., half_dim:], values[..., :half_dim]], -1)
    return values * cosine + rotated * sine

def page_layout(span_counts, prefix_counts, page_count):
    ends = jnp.cumsum(span_counts, axis=1)
    starts = ends - span_counts
    page_index = jnp.arange(page_count, dtype=jnp.int32)
    session_of = lax.optimization_barrier(jnp.sum((page_index[None, :, None] >= ends[:, None, :]).astype(jnp.int32), -1))
    onehot = session_of[..., None] == jnp.arange(span_counts.shape[1], dtype=jnp.int32)
    start_of = lax.optimization_barrier(jnp.sum(jnp.where(onehot, starts[:, None, :], 0), -1))
    prefix_of = lax.optimization_barrier(jnp.sum(jnp.where(onehot, prefix_counts[:, None, :], 0), -1))
    return (session_of, start_of, prefix_of, starts)

def target_ranks(targets):
    count = targets.shape[1]
    order = jnp.arange(count, dtype=jnp.int32)
    earlier = (targets[:, :, None] == targets[:, None, :]) & (order[None, None, :] < order[None, :, None])
    return lax.optimization_barrier(jnp.sum(earlier.astype(jnp.int32), -1))

def key_mask(page_number, start_page, prefix_count, max_pages, most_pages, page_size):
    key_page = jnp.arange(max_pages + most_pages, dtype=jnp.int32)
    relative = page_number - start_page
    within = key_page - max_pages
    query_row = jnp.arange(page_size, dtype=jnp.int32)
    causal = query_row[None, :] <= query_row[:, None]
    prefix_ok = (key_page < prefix_count)[None, :, None]
    span_page = (key_page >= max_pages)[None, :, None]
    earlier = (within < relative)[None, :, None]
    diagonal = (within == relative)[None, :, None] & causal[:, None, :]
    visible = prefix_ok | span_page & (earlier | diagonal)
    visible = jnp.broadcast_to(visible, (page_size, max_pages + most_pages, page_size))
    return visible.reshape(page_size, -1)

def attend(query_page, key_rows, visible):
    page_size, head_count, head_dim = query_page.shape
    group_heads = key_rows.shape[1]
    grouped = query_page.astype(jnp.float32).reshape(page_size, group_heads, -1, head_dim)
    key_part = key_rows[..., :head_dim].astype(jnp.float32)
    value_portion = key_rows[..., head_dim:].astype(jnp.float32)
    scores = jnp.einsum('qhgd,khd->hgqk', grouped, key_part) / jnp.sqrt(jnp.float32(head_dim))
    scores = jnp.where(visible[None, None], scores, -jnp.inf)
    top = lax.optimization_barrier(jnp.max(scores, axis=-1, keepdims=True))
    weights = jnp.exp(scores - top)
    probs = (weights / lax.optimization_barrier(jnp.sum(weights, axis=-1, keepdims=True))).astype(jnp.bfloat16)
    mixed = jnp.einsum('hgqk,khd->qhgd', probs.astype(jnp.float32), value_portion)
    return mixed.astype(jnp.bfloat16).reshape(page_size, -1)

def reference(hidden_in, ln_gain, w_query, key_value_weight, q_gain, k_gain, key_value_cache, prefix_pages, page_holder, page_slot, span_pages, decode_target):
    normalized_input = rms_scale(hidden_in.astype(jnp.float32), ln_gain).astype(jnp.bfloat16)
    query = jnp.dot(normalized_input, w_query, preferred_element_type=jnp.float32).reshape(SPAN_TOKEN_TOTAL, HQ, HEAD_SIZE)
    key_value_rows = jnp.dot(normalized_input, key_value_weight.reshape(MODEL_WIDTH, KEY_VALUE_HEADS * 2 * HEAD_SIZE), preferred_element_type=jnp.float32).reshape(SPAN_TOKEN_TOTAL, KEY_VALUE_HEADS, 2 * HEAD_SIZE)
    session_of, start_of, prefix_of, starts = page_layout(span_pages, prefix_pages, SPAN_PAGES_REP)
    page_index = jnp.arange(SPAN_PAGES_REP, dtype=jnp.int32)
    page_base = (prefix_of + page_index[None, :] - start_of) * PAGE_TOKENS
    positions = (page_base[..., None] + jnp.arange(PAGE_TOKENS, dtype=jnp.int32)).reshape(-1)
    query_rot = rotary(rms_scale(query, q_gain), positions).astype(jnp.bfloat16)
    rotated_key = rotary(rms_scale(key_value_rows[..., :HEAD_SIZE], k_gain), positions).astype(jnp.bfloat16)
    fresh_value_rows = key_value_rows[..., HEAD_SIZE:].astype(jnp.bfloat16)
    incoming_span_pages = jnp.concatenate([rotated_key, fresh_value_rows], -1).reshape(N_REP, SPAN_PAGES_REP, PAGE_TOKENS, KEY_VALUE_HEADS, 2 * HEAD_SIZE)
    query_pages = query_rot.reshape(N_REP, SPAN_PAGES_REP, PAGE_TOKENS, HQ, HEAD_SIZE)
    page_ids = page_holder * PAGES_DEV + page_slot

    def replica_attention(items):
        replica_queries, fresh_pages, replica_numbers, replica_session, replica_start, replica_prefix = items
        fetched_pages = jnp.take(key_value_cache, replica_numbers.reshape(-1), axis=0).reshape(REPLICA_SESSIONS, PREFIX_PAGE_MAX, PAGE_TOKENS, KEY_VALUE_HEADS, 2 * HEAD_SIZE)

        def one_page(page_items):
            page_number, query_page, session, start_page, prefix_count = page_items
            prefix_key_rows = lax.dynamic_index_in_dim(fetched_pages, session, 0, keepdims=False)
            span_ids = jnp.clip(start_page + jnp.arange(MOSTC, dtype=jnp.int32), 0, SPAN_PAGES_REP - 1)
            span_key_rows = jnp.take(fresh_pages, span_ids, axis=0)
            key_rows = jnp.concatenate([prefix_key_rows, span_key_rows], 0).reshape(-1, KEY_VALUE_HEADS, 2 * HEAD_SIZE)
            visible = key_mask(page_number, start_page, prefix_count, PREFIX_PAGE_MAX, MOSTC, PAGE_TOKENS)
            return attend(query_page, key_rows, visible)
        return lax.map(one_page, (page_index, replica_queries, replica_session, replica_start, replica_prefix))
    attn_out = lax.map(replica_attention, (query_pages, incoming_span_pages, page_ids, session_of, start_of, prefix_of))
    attn_out = attn_out.reshape(SPAN_TOKEN_TOTAL, HQ * HEAD_SIZE)
    targets = decode_target[..., 0]
    ranks = target_ranks(targets)
    replica_index = jnp.arange(N_REP, dtype=jnp.int32)
    dest = (targets * N_REP + replica_index[:, None]) * PUSHCAP + ranks
    anchor_ids = replica_index[:, None] * SPAN_PAGES_REP + page_index[None, :]
    anchor = jnp.zeros((NPUSH,), jnp.int32).at[dest.reshape(-1)].set(anchor_ids.reshape(-1).astype(jnp.int32))
    filled = jnp.zeros((NPUSH,), jnp.bool_).at[dest.reshape(-1)].set(True)
    flattened_new = incoming_span_pages.reshape(N_REP * SPAN_PAGES_REP, PAGE_TOKENS, KEY_VALUE_HEADS, 2 * HEAD_SIZE)
    taken = jnp.take(flattened_new, anchor, axis=0)
    pushed = jnp.where(filled[:, None, None, None], taken, jnp.zeros_like(taken))
    return (attn_out, pushed)
```

```python
import functools

import jax
import jax.numpy as jnp
from jax import lax
from jax.experimental import pallas as pl
from jax.experimental.pallas import tpu as pltpu
from jax.sharding import PartitionSpec as P

CHUNK_PAGES = (10, 8, 6)
KEY_BLOCK = 256
VMEM_BYTES = 56 * 1024 * 1024
LOG2E = 1.4426950408889634


def rotary_tables(positions, head_dim):
    half_dim = head_dim // 2
    exponent = jnp.arange(half_dim, dtype=jnp.float32) * (2.0 / head_dim)
    inverse = jnp.power(jnp.float32(1000000.0), -exponent)
    angles = positions.astype(jnp.float32)[:, None] * inverse[None, :]
    cosine, sine = jnp.cos(angles), jnp.sin(angles)
    return jnp.concatenate([cosine, cosine], -1), jnp.concatenate([-sine, sine], -1)


def page_layout(span_counts, prefix_counts, page_count):
    ends = jnp.cumsum(span_counts, axis=0)
    starts = ends - span_counts
    page_index = jnp.arange(page_count, dtype=jnp.int32)
    session_of = jnp.sum((page_index[:, None] >= ends[None, :]).astype(jnp.int32), -1)
    onehot = session_of[:, None] == jnp.arange(span_counts.shape[0], dtype=jnp.int32)
    start_of = jnp.sum(jnp.where(onehot, starts[None, :], 0), -1)
    prefix_of = jnp.sum(jnp.where(onehot, prefix_counts[None, :], 0), -1)
    return session_of, start_of, prefix_of


def target_ranks(targets):
    count = targets.shape[1]
    order = jnp.arange(count, dtype=jnp.int32)
    earlier = (targets[:, :, None] == targets[:, None, :]) & (
        order[None, None, :] < order[None, :, None]
    )
    return jnp.sum(earlier.astype(jnp.int32), -1)


def head_norm_rotary(values, gain, cosine, sine):
    mean_square = jnp.mean(values * values, axis=-1, keepdims=True)
    scaled = values * lax.rsqrt(mean_square + 1e-06) * gain
    return scaled * cosine + pltpu.roll(scaled, values.shape[-1] // 2, axis=1) * sine


def norm_kv_kernel(
    me_ref, own, left, right, far_top, far_low, gain, weight, k_gain, cosine, sine, normed, kv
):
    rows, width = own.shape
    me = me_ref[0]
    half = rows // 2
    tile = 16
    places = [pl.multiple_of(lax.rem(me + shift, 4) * width, 128) for shift in (0, 3, 1, 2)]

    def normalize(start, far, far_start):
        pieces = [
            own[pl.ds(start, tile), :],
            left[pl.ds(start, tile), :],
            right[pl.ds(start, tile), :],
            far[pl.ds(far_start, tile), :],
        ]
        total = jnp.zeros((tile, 128), jnp.float32)
        for piece in pieces:
            wide = piece.astype(jnp.float32)
            square = wide * wide
            for lane in range(0, width, 128):
                total = total + square[:, lane : lane + 128]
        mean_square = jnp.sum(total, axis=-1, keepdims=True) * (1.0 / (4 * width))
        scale = lax.rsqrt(mean_square + 1e-06)
        for piece, place in zip(pieces, places):
            scaled = piece.astype(jnp.float32) * scale * gain[:, pl.ds(place, width)]
            normed[pl.ds(start, tile), pl.ds(place, width)] = scaled.astype(jnp.bfloat16)

    @pl.loop(0, half // tile)
    def _(step):
        start = pl.multiple_of(step * tile, tile)
        normalize(start, far_top, start)

    @pl.loop(0, half // tile)
    def _(step):
        start = pl.multiple_of(step * tile, tile)
        normalize(pl.multiple_of(half + start, tile), far_low, start)

    head_dim = k_gain.shape[1]
    keyval = jnp.dot(normed[...], weight[...], preferred_element_type=jnp.float32)
    key = head_norm_rotary(keyval[:, :head_dim], k_gain[...], cosine[...], sine[...])
    kv[:, :head_dim] = key.astype(jnp.bfloat16)
    kv[:, head_dim:] = keyval[:, head_dim:].astype(jnp.bfloat16)


def norm_kv(me, pieces, gain, weight, k_gain, cosine, sine):
    rows, width = pieces[0].shape
    return pl.pallas_call(
        norm_kv_kernel,
        out_shape=(
            jax.ShapeDtypeStruct((rows, 4 * width), jnp.bfloat16),
            jax.ShapeDtypeStruct((rows, weight.shape[1]), jnp.bfloat16),
        ),
        in_specs=[pl.BlockSpec(memory_space=pltpu.SMEM)]
        + [pl.BlockSpec(memory_space=pltpu.VMEM)] * 10,
        out_specs=[pl.BlockSpec(memory_space=pltpu.VMEM)] * 2,
        compiler_params=pltpu.CompilerParams(vmem_limit_bytes=VMEM_BYTES),
        cost_estimate=pl.CostEstimate(
            flops=2 * rows * 4 * width * weight.shape[1],
            bytes_accessed=16 * rows * width + 8 * width * weight.shape[1],
            transcendentals=0,
        ),
        name="norm_kv",
    )(me, *pieces, gain, weight, k_gain, cosine, sine)


def query_kernel(normed, weight, q_gain, cosine, sine, query):
    head_dim = q_gain.shape[1]
    product = jnp.dot(normed[...], weight[...], preferred_element_type=jnp.float32)
    for start in range(0, product.shape[1], head_dim):
        rotated = head_norm_rotary(
            product[:, start : start + head_dim], q_gain[...], cosine[...], sine[...]
        )
        query[:, start : start + head_dim] = rotated.astype(jnp.bfloat16)


def project_query(normed, weight, q_gain, cosine, sine):
    rows, depth = normed.shape
    columns = weight.shape[1]
    tile = 256
    whole = lambda shape: pl.BlockSpec(shape, lambda n: (0, 0))
    return pl.pallas_call(
        query_kernel,
        grid=(columns // tile,),
        out_shape=jax.ShapeDtypeStruct((rows, columns), jnp.bfloat16),
        in_specs=[
            whole((rows, depth)),
            pl.BlockSpec((depth, tile), lambda n: (0, n)),
            whole(q_gain.shape),
            whole(cosine.shape),
            whole(sine.shape),
        ],
        out_specs=pl.BlockSpec((rows, tile), lambda n: (0, n)),
        compiler_params=pltpu.CompilerParams(vmem_limit_bytes=VMEM_BYTES),
        cost_estimate=pl.CostEstimate(
            flops=2 * rows * depth * columns,
            bytes_accessed=2 * (rows * depth + depth * columns + rows * columns),
            transcendentals=0,
        ),
        name="query",
    )(normed, weight, q_gain, cosine, sine)


def attention_kernel(
    page_base, chunk_count, session, start, prefix, query, prefix_kv, *refs
):
    kv_chunks = refs[:chunk_count]
    out, span = refs[-2:]
    step = pl.program_id(0)
    page = page_base + step
    head_dim = prefix_kv.shape[1] // 2
    page_size = query.shape[0]
    heads = query.shape[1] // head_dim
    rows = heads * page_size
    block_pages = KEY_BLOCK // page_size

    @pl.when(step == 0)
    def _():
        filled = 0
        for chunk in kv_chunks:
            span[pl.ds(filled, chunk.shape[0]), :] = chunk[...]
            filled += chunk.shape[0]
        if filled < span.shape[0]:
            span[filled:, :] = jnp.zeros((span.shape[0] - filled, span.shape[1]), span.dtype)

    grouped = jnp.concatenate(
        [query[:, h * head_dim : (h + 1) * head_dim] for h in range(heads)], axis=0
    )
    factor = LOG2E / float(head_dim) ** 0.5
    my_prefix = prefix[page]
    my_start = start[page]
    prefix_base = session[page] * (prefix_kv.shape[0] // 4)
    column = lax.broadcasted_iota(jnp.int32, (rows, KEY_BLOCK), 1)
    token = lax.broadcasted_iota(jnp.int32, (rows, KEY_BLOCK), 0) & (page_size - 1)

    def update(carry, keys_values, visible):
        top, total, mixed = carry
        scores = lax.dot_general(
            grouped,
            keys_values[:, :head_dim],
            (((1,), (1,)), ((), ())),
            preferred_element_type=jnp.float32,
        )
        scores = jnp.where(visible, scores * factor, -jnp.inf)
        new_top = jnp.maximum(top, jnp.max(scores, axis=-1, keepdims=True))
        weights = jnp.exp2(scores - new_top)
        fade = jnp.exp2(top - new_top)
        total = total * fade + jnp.sum(weights, axis=-1, keepdims=True)
        mixed = mixed * fade + jnp.dot(
            weights.astype(jnp.bfloat16),
            keys_values[:, head_dim:],
            preferred_element_type=jnp.float32,
        )
        return new_top, total, mixed

    def prefix_block(block, carry):
        base = pl.multiple_of(block * KEY_BLOCK, KEY_BLOCK)
        rows_at = pl.multiple_of(prefix_base + base, KEY_BLOCK)
        visible = column < my_prefix * page_size - base
        return update(carry, prefix_kv[pl.ds(rows_at, KEY_BLOCK), :], visible)

    def span_block(block, carry):
        base = my_start * page_size + block * KEY_BLOCK
        rows_at = pl.multiple_of(jnp.minimum(base, span.shape[0] - KEY_BLOCK), page_size)
        absolute = column + rows_at
        visible = (absolute >= base) & (absolute <= page * page_size + token)
        return update(carry, span[pl.ds(rows_at, KEY_BLOCK), :], visible)

    carry = (
        jnp.full((rows, 1), -jnp.inf, jnp.float32),
        jnp.zeros((rows, 1), jnp.float32),
        jnp.zeros((rows, head_dim), jnp.float32),
    )
    carry = lax.fori_loop(
        0, lax.div(my_prefix + (block_pages - 1), block_pages), prefix_block, carry
    )
    span_count = lax.div(page - my_start + block_pages, block_pages)
    carry = lax.fori_loop(0, span_count, span_block, carry)
    mixed = (carry[2] / carry[1]).astype(jnp.bfloat16)
    for h in range(heads):
        out[:, h * head_dim : (h + 1) * head_dim] = mixed[h * page_size : (h + 1) * page_size]


def attention(page_base, layout, query, prefix_kv, kv_chunks, previous, row_count, page_size):
    rows, columns = query.shape
    pages = rows // page_size
    whole = lambda shape: pl.BlockSpec(shape, lambda p, *_: (0, 0))
    operands = [query, prefix_kv, *kv_chunks]
    in_specs = [pl.BlockSpec((page_size, columns), lambda p, *_: (p, 0))]
    in_specs += [whole(operand.shape) for operand in operands[1:]]
    aliases = {}
    if previous is not None:
        aliases = {len(layout) + len(operands): 0}
        operands.append(previous)
        in_specs.append(pl.BlockSpec(memory_space=pl.ANY))
    return pl.pallas_call(
        functools.partial(attention_kernel, page_base, len(kv_chunks)),
        grid_spec=pltpu.PrefetchScalarGridSpec(
            num_scalar_prefetch=len(layout),
            grid=(pages,),
            in_specs=in_specs,
            out_specs=pl.BlockSpec((page_size, columns), lambda p, *_: (page_base + p, 0)),
            scratch_shapes=[pltpu.VMEM((row_count, prefix_kv.shape[1]), jnp.bfloat16)],
        ),
        out_shape=jax.ShapeDtypeStruct((row_count, columns), jnp.bfloat16),
        input_output_aliases=aliases,
        compiler_params=pltpu.CompilerParams(vmem_limit_bytes=VMEM_BYTES),
        cost_estimate=pl.CostEstimate(
            flops=4 * rows * columns * 1200,
            bytes_accessed=4 * rows * columns + 6 * prefix_kv.size,
            transcendentals=rows * 8 * 1200,
        ),
        name="attention",
    )(*layout, *operands)


def per_device(
    hidden_in,
    ln_gain,
    w_query,
    key_value_weight,
    q_gain,
    k_gain,
    key_value_cache,
    prefix_pages,
    page_holder,
    page_slot,
    span_pages,
    decode_target,
):
    replica = lax.axis_index("rep")
    me = lax.axis_index("tp").astype(jnp.int32)
    replicas = lax.axis_size("rep")
    parts = lax.axis_size("tp")
    up = [(i, (i + 1) % parts) for i in range(parts)]
    down = [(i, (i - 1) % parts) for i in range(parts)]
    head_dim = q_gain.shape[0]
    page_size = key_value_cache.shape[1]
    row_count = hidden_in.shape[0]
    page_count = row_count // page_size
    sessions = span_pages.shape[1]
    max_pages = page_holder.shape[2]
    capacity = sessions * max_pages // replicas
    push_slots = 2

    pieces = []
    row = 0
    for pages in CHUNK_PAGES:
        rows = pages * page_size
        own = hidden_in[row : row + rows]
        left = lax.ppermute(own, "tp", up)
        right = lax.ppermute(own, "tp", down)
        pieces.append((own, left, right))
        row += rows
    chunks = []
    for own, left, right in pieces:
        half = own.shape[0] // 2
        far_top = lax.ppermute(left[:half], "tp", up)
        far_low = lax.ppermute(right[half:], "tp", down)
        chunks.append((own, left, right, far_top, far_low))

    position_count = sessions * max_pages
    flat_holder = page_holder.reshape(replicas, position_count)
    flat_slot = page_slot.reshape(replicas, position_count)
    from_here = flat_holder == replica
    send_rank = jnp.cumsum(from_here.astype(jnp.int32), axis=1) - 1
    slot_range = jnp.arange(capacity, dtype=jnp.int32)
    matched = from_here[:, None, :] & (send_rank[:, None, :] == slot_range[None, :, None])
    local_ids = jnp.sum(jnp.where(matched, flat_slot[:, None, :], 0), -1)
    cache = key_value_cache.reshape(-1, page_size, 2 * head_dim)
    outgoing = jnp.take(cache, local_ids.reshape(-1), axis=0, mode="clip")
    outgoing = outgoing.reshape(replicas, capacity, page_size, 2 * head_dim)
    incoming = lax.all_to_all(outgoing, "rep", split_axis=0, concat_axis=0, tiled=True)
    incoming = incoming.reshape(replicas * capacity, page_size, 2 * head_dim)
    my_holder = lax.dynamic_index_in_dim(flat_holder, replica, 0, keepdims=False)
    position_index = jnp.arange(position_count, dtype=jnp.int32)
    same_earlier = (my_holder[:, None] == my_holder[None, :]) & (
        position_index[None, :] < position_index[:, None]
    )
    recv_rank = jnp.sum(same_earlier.astype(jnp.int32), axis=1)
    recv_ids = my_holder * capacity + recv_rank
    prefix_kv = jnp.take(incoming, recv_ids, axis=0, mode="clip")
    prefix_kv = prefix_kv.reshape(position_count * page_size, 2 * head_dim)

    my_span = lax.dynamic_index_in_dim(span_pages, replica, 0, keepdims=False)
    my_prefix = lax.dynamic_index_in_dim(prefix_pages, replica, 0, keepdims=False)
    layout = page_layout(my_span, my_prefix, page_count)
    session_of, start_of, prefix_of = layout
    page_index = jnp.arange(page_count, dtype=jnp.int32)
    page_first = (prefix_of + page_index - start_of) * page_size
    positions = (page_first[:, None] + jnp.arange(page_size, dtype=jnp.int32)[None, :]).reshape(-1)
    cosine, sine = rotary_tables(positions, head_dim)

    targets = decode_target[..., 0]
    my_targets = lax.dynamic_index_in_dim(targets, replica, 0, keepdims=True)
    my_ranks = target_ranks(my_targets)[0]
    wanted = jnp.arange(replicas * push_slots, dtype=jnp.int32)
    chosen = (my_targets[0] * push_slots + my_ranks)[None, :] == wanted[:, None]
    push_ids = jnp.sum(jnp.where(chosen, page_index[None, :], 0), -1)
    push_valid = jnp.any(chosen, axis=-1)

    gain = ln_gain.reshape(1, -1)
    kv_weight = key_value_weight.reshape(key_value_weight.shape[0], -1)
    q_gain, k_gain = q_gain.reshape(1, -1), k_gain.reshape(1, -1)
    kv_chunks = []
    attn_out = None
    row = 0
    for index, chunk in enumerate(chunks):
        rows = chunk[0].shape[0]
        cos_rows, sin_rows = cosine[row : row + rows], sine[row : row + rows]
        normed, kv = norm_kv(me[None], chunk, gain, kv_weight, k_gain, cos_rows, sin_rows)
        kv_chunks.append(kv)
        if index == len(chunks) - 1:
            fresh = jnp.concatenate(kv_chunks, 0).reshape(page_count, page_size, 2 * head_dim)
            pushing = jnp.take(fresh, push_ids, axis=0, mode="clip")
            pushing = jnp.where(push_valid[:, None, None], pushing, jnp.zeros_like(pushing))
            pushing = pushing.reshape(replicas, push_slots, page_size, 2 * head_dim)
            pushed = lax.all_to_all(pushing, "rep", split_axis=0, concat_axis=0, tiled=True)
        query = project_query(normed, w_query, q_gain, cos_rows, sin_rows)
        attn_out = attention(
            row // page_size, layout, query, prefix_kv, kv_chunks, attn_out, row_count, page_size
        )
        row += rows
    pushed = pushed.reshape(replicas * push_slots, page_size, 1, 2 * head_dim)
    return (attn_out, pushed)


def solution(mesh):
    placed = (
        P("rep", "tp"),
        P(),
        P(None, "tp"),
        P(None, "tp", None),
        P(),
        P(),
        P("rep", None, "tp", None),
        P(),
        P(),
        P(),
        P(),
        P(),
    )
    return jax.shard_map(
        per_device,
        mesh=mesh,
        in_specs=placed,
        out_specs=(P("rep", "tp"), P("rep", None, "tp", None)),
        check_vma=False,
    )
```

```python
import functools

import jax
import jax.numpy as jnp
from jax import lax
from jax.experimental import pallas as pl
from jax.experimental.pallas import tpu as pltpu
from jax.sharding import PartitionSpec as P

CHUNK_PAGES = (4, 6, 8, 6)
GROUPS = 1
SPAN_STEP = 4
VMEM_BYTES = 56 * 1024 * 1024
TINY_COST = pl.CostEstimate(flops=1, bytes_accessed=1, transcendentals=0)
LOG2E = 1.4426950408889634


def rotary_tables(positions, head_dim):
    half_dim = head_dim // 2
    exponent = jnp.arange(half_dim, dtype=jnp.float32) * (2.0 / head_dim)
    inverse = jnp.power(jnp.float32(1000000.0), -exponent)
    angles = positions.astype(jnp.float32)[:, None] * inverse[None, :]
    cosine, sine = jnp.cos(angles), jnp.sin(angles)
    return jnp.concatenate([cosine, cosine], -1), jnp.concatenate([-sine, sine], -1)


def page_layout(span_counts, prefix_counts, page_count):
    ends = jnp.cumsum(span_counts, axis=0)
    starts = ends - span_counts
    page_index = jnp.arange(page_count, dtype=jnp.int32)
    session_of = jnp.sum((page_index[:, None] >= ends[None, :]).astype(jnp.int32), -1)
    onehot = session_of[:, None] == jnp.arange(span_counts.shape[0], dtype=jnp.int32)
    start_of = jnp.sum(jnp.where(onehot, starts[None, :], 0), -1)
    prefix_of = jnp.sum(jnp.where(onehot, prefix_counts[None, :], 0), -1)
    return session_of, start_of, prefix_of


def target_ranks(targets):
    count = targets.shape[1]
    order = jnp.arange(count, dtype=jnp.int32)
    earlier = (targets[:, :, None] == targets[:, None, :]) & (
        order[None, None, :] < order[None, :, None]
    )
    return jnp.sum(earlier.astype(jnp.int32), -1)


def head_norm_rotary(values, ones, gain, cosine, sine):
    square = values * values
    high = square.astype(jnp.bfloat16)
    low = (square - high.astype(jnp.float32)).astype(jnp.bfloat16)
    mean_square = jnp.dot(high, ones, preferred_element_type=jnp.float32)
    mean_square = mean_square + jnp.dot(low, ones, preferred_element_type=jnp.float32)
    scaled = values * lax.rsqrt(mean_square + 1e-06)
    head_dim = gain.shape[1]
    heads = []
    for start in range(0, values.shape[1], head_dim):
        head = scaled[:, start : start + head_dim] * gain
        heads.append(head * cosine + pltpu.roll(head, head_dim // 2, axis=1) * sine)
    return heads


def head_mean(columns, head_dim):
    column = lax.broadcasted_iota(jnp.int32, (columns, columns), 1)
    row = lax.broadcasted_iota(jnp.int32, (columns, columns), 0)
    same = lax.div(row, head_dim) == lax.div(column, head_dim)
    return jnp.where(same, 1.0 / head_dim, 0.0).astype(jnp.bfloat16)


def norm_kv_kernel(
    me_ref, own, left, right, far_top, far_low, gain, weight, k_gain, cosine, sine, *refs
):
    normed, kv = refs[-2:]
    rows, width = own.shape
    me = me_ref[0]
    tile = 64
    places = [pl.multiple_of(lax.rem(me + shift, 4) * width, 128) for shift in (0, 3, 1, 2)]

    def normalize(far):
        @pl.loop(0, rows // tile)
        def _(step):
            at = pl.ds(pl.multiple_of(step * tile, tile), tile)
            pieces = [own, left, right, far]
            total = jnp.zeros((tile, 128), jnp.float32)
            for piece in pieces:
                wide = piece[at, :].astype(jnp.float32)
                square = wide * wide
                for lane in range(0, width, 128):
                    total = total + square[:, lane : lane + 128]
            mean_square = jnp.sum(total, axis=-1, keepdims=True) * (1.0 / (4 * width))
            scale = lax.rsqrt(mean_square + 1e-06)
            for piece, place in zip(pieces, places):
                scaled = piece[at, :].astype(jnp.float32) * scale * gain[:, pl.ds(place, width)]
                normed[at, pl.ds(place, width)] = scaled.astype(jnp.bfloat16)

    @pl.when(pl.program_id(0) == 0)
    def _():
        normalize(far_top)

    @pl.when(pl.program_id(0) == 1)
    def _():
        normalize(far_low)

    head_dim = k_gain.shape[1]
    keyval = jnp.dot(normed[...], weight[...], preferred_element_type=jnp.float32)
    ones = head_mean(head_dim, head_dim)
    keys = keyval[:, :head_dim]
    key = head_norm_rotary(keys, ones, k_gain[...], cosine[...], sine[...])[0]
    kv[:, :head_dim] = key.astype(jnp.bfloat16)
    kv[:, head_dim:] = keyval[:, head_dim:].astype(jnp.bfloat16)


def norm_kv(me, pieces, gain, weight, k_gain, cosine, sine, after):
    rows, width = pieces[0].shape
    half = rows // 2
    whole = lambda shape: pl.BlockSpec(shape, lambda i: (0, 0))
    split = lambda columns: pl.BlockSpec((half, columns), lambda i: (i, 0))
    return pl.pallas_call(
        norm_kv_kernel,
        grid=(2,),
        out_shape=(
            jax.ShapeDtypeStruct((rows, 4 * width), jnp.bfloat16),
            jax.ShapeDtypeStruct((rows, weight.shape[1]), jnp.bfloat16),
        ),
        in_specs=[
            pl.BlockSpec(memory_space=pltpu.SMEM),
            split(width),
            split(width),
            split(width),
            whole((half, width)),
            whole((half, width)),
            whole(gain.shape),
            whole(weight.shape),
            whole(k_gain.shape),
            split(cosine.shape[1]),
            split(sine.shape[1]),
        ]
        + [pl.BlockSpec(memory_space=pl.ANY)] * len(after),
        out_specs=[split(4 * width), split(weight.shape[1])],
        compiler_params=pltpu.CompilerParams(vmem_limit_bytes=VMEM_BYTES),
        cost_estimate=TINY_COST,
        name="norm_kv",
    )(me, *pieces, gain, weight, k_gain, cosine, sine, *after)


def query_kernel(normed, weight, q_gain, cosine, sine, *refs):
    query = refs[-1]
    head_dim = q_gain.shape[1]
    product = jnp.dot(normed[...], weight[...], preferred_element_type=jnp.float32)
    ones = head_mean(product.shape[1], head_dim)
    heads = head_norm_rotary(product, ones, q_gain[...], cosine[...], sine[...])
    for index, head in enumerate(heads):
        query[:, index * head_dim : (index + 1) * head_dim] = head.astype(jnp.bfloat16)


def project_query(normed, weight, q_gain, cosine, sine, after):
    rows, depth = normed.shape
    columns = weight.shape[1]
    tile = 256
    whole = lambda shape: pl.BlockSpec(shape, lambda n: (0, 0))
    return pl.pallas_call(
        query_kernel,
        grid=(columns // tile,),
        out_shape=jax.ShapeDtypeStruct((rows, columns), jnp.bfloat16),
        in_specs=[
            whole((rows, depth)),
            pl.BlockSpec((depth, tile), lambda n: (0, n)),
            whole(q_gain.shape),
            whole(cosine.shape),
            whole(sine.shape),
        ]
        + [pl.BlockSpec(memory_space=pl.ANY)] * len(after),
        out_specs=pl.BlockSpec((rows, tile), lambda n: (0, n)),
        compiler_params=pltpu.CompilerParams(vmem_limit_bytes=VMEM_BYTES),
        cost_estimate=TINY_COST,
        name="query",
    )(normed, weight, q_gain, cosine, sine, *after)


def forward_kernel(starts, after_count, *refs):
    count = len(starts)
    sources, outs, sems = refs[:count], refs[count + after_count : -1], refs[-1]
    copies = [
        pltpu.make_async_copy(source.at[pl.ds(start, out.shape[0]), :], out, sems.at[index])
        for index, (source, start, out) in enumerate(zip(sources, starts, outs))
    ]
    for copy in copies:
        copy.start()
    for copy in copies:
        copy.wait()


def take_rows(pieces, after):
    sources = [piece[0] for piece in pieces]
    return pl.pallas_call(
        functools.partial(forward_kernel, [piece[1] for piece in pieces], len(after)),
        out_shape=[
            jax.ShapeDtypeStruct((rows, source.shape[1]), source.dtype)
            for source, _, rows in pieces
        ],
        in_specs=[pl.BlockSpec(memory_space=pl.ANY)] * (len(sources) + len(after)),
        out_specs=[pl.BlockSpec(memory_space=pltpu.VMEM)] * len(pieces),
        scratch_shapes=[pltpu.SemaphoreType.DMA((len(pieces),))],
        compiler_params=pltpu.CompilerParams(vmem_limit_bytes=VMEM_BYTES),
        cost_estimate=TINY_COST,
        name="take_rows",
    )(*sources, *after)


def attention_kernel(
    page_base, chunk_count, session, start, prefix, query, prefix_kv, *refs
):
    kv_chunks = refs[:chunk_count]
    out, span = refs[-2:]
    step = pl.program_id(0)
    page = page_base + step
    head_dim = prefix_kv.shape[1] // 2
    page_size = query.shape[0]
    heads = query.shape[1] // head_dim
    rows = heads * page_size

    @pl.when(step == 0)
    def _():
        filled = 0
        for chunk in kv_chunks:
            span[pl.ds(filled, chunk.shape[0]), :] = chunk[...]
            filled += chunk.shape[0]
        if filled < span.shape[0]:
            span[filled:, :] = jnp.zeros((span.shape[0] - filled, span.shape[1]), span.dtype)

    split = rows // GROUPS
    grouped = jnp.concatenate(
        [query[:, h * head_dim : (h + 1) * head_dim] for h in range(heads)], axis=0
    )
    grouped = grouped.T
    groups = [grouped[:, g * split : (g + 1) * split] for g in range(GROUPS)]
    factor = LOG2E / float(head_dim) ** 0.5
    my_prefix = prefix[page]
    my_start = start[page]
    lanes = 128

    def key_index(count):
        return lax.broadcasted_iota(jnp.int32, (count, lanes), 0)

    def attend(span_rows):
        prefix_rows = prefix_kv.shape[0] // 4
        prefix_at = pl.multiple_of(session[page] * prefix_rows, prefix_rows)
        first = my_start * page_size
        span_at = pl.multiple_of(jnp.minimum(first, span.shape[0] - span_rows), page_size)
        token = lax.broadcasted_iota(jnp.int32, (span_rows, lanes), 1) & (page_size - 1)
        absolute = key_index(span_rows) + span_at
        parts = [
            (
                prefix_kv[pl.ds(prefix_at, prefix_rows), :],
                key_index(prefix_rows) < my_prefix * page_size,
            ),
            (
                span[pl.ds(span_at, span_rows), :],
                (absolute >= first) & (absolute <= page * page_size + token),
            ),
        ]
        biases = [
            jnp.concatenate([jnp.where(visible, 0.0, -jnp.inf)] * (split // lanes), axis=1)
            for _, visible in parts
        ]
        for g, group in enumerate(groups):
            scores = [
                jnp.dot(rows[:, :head_dim], group, preferred_element_type=jnp.float32) + bias
                for (rows, _), bias in zip(parts, biases)
            ]
            top = [jnp.max(score, axis=0, keepdims=True) for score in scores]
            top = jnp.maximum(top[0], top[1]) * factor
            weights = [jnp.exp2(score * factor - top) for score in scores]
            total = sum(jnp.sum(weight, axis=0, keepdims=True) for weight in weights)
            inverse = 1.0 / total
            mixed = sum(
                lax.dot_general(
                    rows[:, head_dim:],
                    (weight * inverse).astype(jnp.bfloat16),
                    (((0,), (0,)), ((), ())),
                    preferred_element_type=jnp.float32,
                )
                for (rows, _), weight in zip(parts, weights)
            )
            mixed = mixed.T.astype(jnp.bfloat16)
            for part in range(split // page_size):
                h = g * (split // page_size) + part
                out[:, h * head_dim : (h + 1) * head_dim] = mixed[
                    part * page_size : (part + 1) * page_size
                ]

    pages_seen = page - my_start + 1
    most = span.shape[0] // (2 * page_size)
    for low in range(0, most, SPAN_STEP):

        @pl.when((pages_seen > low) & (pages_seen <= low + SPAN_STEP))
        def _():
            attend((low + SPAN_STEP) * page_size)


def attention(
    page_base, layout, query, prefix_kv, kv_chunks, previous, row_count, page_size, after
):
    rows, columns = query.shape
    pages = rows // page_size
    whole = lambda shape: pl.BlockSpec(shape, lambda p, *_: (0, 0))
    operands = [query, prefix_kv, *kv_chunks]
    in_specs = [pl.BlockSpec((page_size, columns), lambda p, *_: (p, 0))]
    in_specs += [whole(operand.shape) for operand in operands[1:]]
    aliases = {}
    if previous is not None:
        aliases = {len(layout) + len(operands): 0}
        operands.append(previous)
        in_specs.append(pl.BlockSpec(memory_space=pl.ANY))
    operands += after
    in_specs += [pl.BlockSpec(memory_space=pl.ANY)] * len(after)
    return pl.pallas_call(
        functools.partial(attention_kernel, page_base, len(kv_chunks)),
        grid_spec=pltpu.PrefetchScalarGridSpec(
            num_scalar_prefetch=len(layout),
            grid=(pages,),
            in_specs=in_specs,
            out_specs=pl.BlockSpec((page_size, columns), lambda p, *_: (page_base + p, 0)),
            scratch_shapes=[pltpu.VMEM((row_count, prefix_kv.shape[1]), jnp.bfloat16)],
        ),
        out_shape=jax.ShapeDtypeStruct((row_count, columns), jnp.bfloat16),
        input_output_aliases=aliases,
        compiler_params=pltpu.CompilerParams(vmem_limit_bytes=VMEM_BYTES),
        cost_estimate=TINY_COST,
        name="attention",
    )(*layout, *operands)


def per_device(
    hidden_in,
    ln_gain,
    w_query,
    key_value_weight,
    q_gain,
    k_gain,
    key_value_cache,
    prefix_pages,
    page_holder,
    page_slot,
    span_pages,
    decode_target,
):
    replica = lax.axis_index("rep")
    me = lax.axis_index("tp").astype(jnp.int32)
    replicas = lax.axis_size("rep")
    parts = lax.axis_size("tp")
    up = [(i, (i + 1) % parts) for i in range(parts)]
    down = [(i, (i - 1) % parts) for i in range(parts)]
    head_dim = q_gain.shape[0]
    page_size = key_value_cache.shape[1]
    row_count = hidden_in.shape[0]
    page_count = row_count // page_size
    sessions = span_pages.shape[1]
    max_pages = page_holder.shape[2]
    capacity = sessions * max_pages // replicas
    push_slots = 2

    position_count = sessions * max_pages
    flat_holder = page_holder.reshape(replicas, position_count)
    flat_slot = page_slot.reshape(replicas, position_count)
    from_here = flat_holder == replica
    send_rank = jnp.cumsum(from_here.astype(jnp.int32), axis=1) - 1
    slot_range = jnp.arange(capacity, dtype=jnp.int32)
    matched = from_here[:, None, :] & (send_rank[:, None, :] == slot_range[None, :, None])
    local_ids = jnp.sum(jnp.where(matched, flat_slot[:, None, :], 0), -1)
    cache = key_value_cache.reshape(-1, page_size, 2 * head_dim)
    outgoing = jnp.take(cache, local_ids.reshape(-1), axis=0, mode="clip")
    outgoing = outgoing.reshape(replicas, capacity, page_size, 2 * head_dim)
    incoming = lax.all_to_all(outgoing, "rep", split_axis=0, concat_axis=0, tiled=True)
    incoming = incoming.reshape(replicas * capacity, page_size, 2 * head_dim)
    my_holder = lax.dynamic_index_in_dim(flat_holder, replica, 0, keepdims=False)
    position_index = jnp.arange(position_count, dtype=jnp.int32)
    same_earlier = (my_holder[:, None] == my_holder[None, :]) & (
        position_index[None, :] < position_index[:, None]
    )
    recv_rank = jnp.sum(same_earlier.astype(jnp.int32), axis=1)
    recv_ids = my_holder * capacity + recv_rank
    prefix_kv = jnp.take(incoming, recv_ids, axis=0, mode="clip")
    prefix_kv = prefix_kv.reshape(position_count * page_size, 2 * head_dim)

    my_span = lax.dynamic_index_in_dim(span_pages, replica, 0, keepdims=False)
    my_prefix = lax.dynamic_index_in_dim(prefix_pages, replica, 0, keepdims=False)
    layout = page_layout(my_span, my_prefix, page_count)
    session_of, start_of, prefix_of = layout
    page_index = jnp.arange(page_count, dtype=jnp.int32)
    page_first = (prefix_of + page_index - start_of) * page_size
    positions = (page_first[:, None] + jnp.arange(page_size, dtype=jnp.int32)[None, :]).reshape(-1)
    cosine, sine = rotary_tables(positions, head_dim)

    targets = decode_target[..., 0]
    my_targets = lax.dynamic_index_in_dim(targets, replica, 0, keepdims=True)
    my_ranks = target_ranks(my_targets)[0]
    wanted = jnp.arange(replicas * push_slots, dtype=jnp.int32)
    chosen = (my_targets[0] * push_slots + my_ranks)[None, :] == wanted[:, None]
    push_ids = jnp.sum(jnp.where(chosen, page_index[None, :], 0), -1)
    push_valid = jnp.any(chosen, axis=-1).astype(jnp.int32)

    gain = ln_gain.reshape(1, -1)
    kv_weight = key_value_weight.reshape(key_value_weight.shape[0], -1)
    q_gain, k_gain = q_gain.reshape(1, -1), k_gain.reshape(1, -1)
    count = len(CHUNK_PAGES)
    sizes = [pages * page_size for pages in CHUNK_PAGES]
    offsets = [sum(sizes[:index]) for index in range(count)]
    own, near, far = {}, {}, {}

    def send_near(index, rows):
        own[index] = rows
        near[index] = lax.ppermute(rows, "tp", up), lax.ppermute(rows, "tp", down)

    def send_far(index, after):
        half = sizes[index] // 2
        left, right = near[index]
        pieces = [(left, 0, half), (right, half, half)]
        following = index + 1 if index else count
        if following < count:
            pieces.append((hidden_in, offsets[following], sizes[following]))
        copies = take_rows(pieces, after)
        far[index] = lax.ppermute(copies[0], "tp", up), lax.ppermute(copies[1], "tp", down)
        if following < count:
            send_near(following, copies[2])
        return copies[0]

    for index in range(2):
        send_near(index, hidden_in[offsets[index] : offsets[index] + sizes[index]])
    send_far(0, [])
    last = [send_far(1, [*far[0], cosine, sine, push_ids, push_valid]), prefix_kv]
    kv_chunks, normed, attn_out = [], {}, None

    def rows_of(table, index):
        return table[offsets[index] : offsets[index] + sizes[index]]

    def run_keys(index, last):
        chunk = (own[index], *near[index], *far[index])
        tables = rows_of(cosine, index), rows_of(sine, index)
        normed[index], kv = norm_kv(me[None], chunk, gain, kv_weight, k_gain, *tables, last)
        kv_chunks.append(kv)
        return [kv]

    def run_query(index, last):
        tables = rows_of(cosine, index), rows_of(sine, index)
        return project_query(normed[index], w_query, q_gain, *tables, last)

    def run_attention(index, query, previous, last):
        return attention(
            offsets[index] // page_size,
            layout,
            query,
            prefix_kv,
            kv_chunks[: index + 1],
            previous,
            row_count,
            page_size,
            last,
        )

    for index in range(count - 1):
        last = run_keys(index, last)
        if index:
            last = [send_far(index + 1, last)]
        query = run_query(index, last)
        last = [query]
        if index < count - 2:
            attn_out = run_attention(index, query, attn_out, last)
            last = [attn_out]
    last = run_keys(count - 1, last)
    fresh = jnp.concatenate(kv_chunks, 0).reshape(page_count, page_size, 2 * head_dim)
    pushing = jnp.take(fresh, push_ids, axis=0, mode="clip")
    pushing = jnp.where(push_valid[:, None, None] > 0, pushing, jnp.zeros_like(pushing))
    pushing = pushing.reshape(replicas, push_slots, page_size, 2 * head_dim)
    pushed = lax.all_to_all(pushing, "rep", split_axis=0, concat_axis=0, tiled=True)
    attn_out = run_attention(count - 2, query, attn_out, [pushing])
    query = run_query(count - 1, [attn_out])
    attn_out = run_attention(count - 1, query, attn_out, [])
    pushed = pushed.reshape(replicas * push_slots, page_size, 1, 2 * head_dim)
    return (attn_out, pushed)


def solution(mesh):
    placed = (
        P("rep", "tp"),
        P(),
        P(None, "tp"),
        P(None, "tp", None),
        P(),
        P(),
        P("rep", None, "tp", None),
        P(),
        P(),
        P(),
        P(),
        P(),
    )
    return jax.shard_map(
        per_device,
        mesh=mesh,
        in_specs=placed,
        out_specs=(P("rep", "tp"), P("rep", None, "tp", None)),
        check_vma=False,
    )
```

```python
import functools

import jax
import jax.numpy as jnp
from jax import lax
from jax.experimental import pallas as pl
from jax.experimental.pallas import tpu as pltpu
from jax.sharding import PartitionSpec as P

CHUNK_PAGES = (8, 8, 8)
GROUPS = 1
NORM_ROWS = 32
SPAN_STEP = 4
VMEM_BYTES = 56 * 1024 * 1024
TINY_COST = pl.CostEstimate(flops=1, bytes_accessed=1, transcendentals=0)
LOG2E = 1.4426950408889634


def rotary_tables(positions, head_dim):
    half_dim = head_dim // 2
    exponent = jnp.arange(half_dim, dtype=jnp.float32) * (2.0 / head_dim)
    inverse = jnp.power(jnp.float32(1000000.0), -exponent)
    angles = positions.astype(jnp.float32)[:, None] * inverse[None, :]
    cosine, sine = jnp.cos(angles), jnp.sin(angles)
    return jnp.concatenate([cosine, cosine], -1), jnp.concatenate([-sine, sine], -1)


def page_layout(span_counts, prefix_counts, page_count):
    ends = jnp.cumsum(span_counts, axis=0)
    starts = ends - span_counts
    page_index = jnp.arange(page_count, dtype=jnp.int32)
    session_of = jnp.sum((page_index[:, None] >= ends[None, :]).astype(jnp.int32), -1)
    onehot = session_of[:, None] == jnp.arange(span_counts.shape[0], dtype=jnp.int32)
    start_of = jnp.sum(jnp.where(onehot, starts[None, :], 0), -1)
    prefix_of = jnp.sum(jnp.where(onehot, prefix_counts[None, :], 0), -1)
    return session_of, start_of, prefix_of


def target_ranks(targets):
    count = targets.shape[1]
    order = jnp.arange(count, dtype=jnp.int32)
    earlier = (targets[:, :, None] == targets[:, None, :]) & (
        order[None, None, :] < order[None, :, None]
    )
    return jnp.sum(earlier.astype(jnp.int32), -1)


def head_norm_rotary(values, ones, gain, cosine, sine):
    square = values * values
    high = square.astype(jnp.bfloat16)
    low = (square - high.astype(jnp.float32)).astype(jnp.bfloat16)
    mean_square = jnp.dot(high, ones, preferred_element_type=jnp.float32)
    mean_square = mean_square + jnp.dot(low, ones, preferred_element_type=jnp.float32)
    scaled = values * lax.rsqrt(mean_square + 1e-06)
    head_dim = gain.shape[1]
    heads = []
    for start in range(0, values.shape[1], head_dim):
        head = scaled[:, start : start + head_dim] * gain
        heads.append(head * cosine + pltpu.roll(head, head_dim // 2, axis=1) * sine)
    return heads


def head_mean(columns, head_dim):
    column = lax.broadcasted_iota(jnp.int32, (columns, columns), 1)
    row = lax.broadcasted_iota(jnp.int32, (columns, columns), 0)
    same = lax.div(row, head_dim) == lax.div(column, head_dim)
    return jnp.where(same, 1.0 / head_dim, 0.0).astype(jnp.bfloat16)


def project_kernel(
    me_ref,
    own,
    left,
    right,
    far_top,
    far_low,
    gain,
    kv_weight,
    q_weight,
    k_gain,
    q_gain,
    cosine,
    sine,
    *refs,
):
    query, kv, normed = refs[-3:]
    rows, width = own.shape
    half = rows // 2
    head_dim = k_gain.shape[1]

    @pl.when(pl.program_id(0) == 0)
    def _():
        me = me_ref[0]
        tile = NORM_ROWS
        places = [pl.multiple_of(lax.rem(me + shift, 4) * width, 128) for shift in (0, 3, 1, 2)]

        def normalize(start, far, far_start):
            at = pl.ds(start, tile)
            pieces = [own[at, :], left[at, :], right[at, :], far[pl.ds(far_start, tile), :]]
            total = jnp.zeros((tile, 128), jnp.float32)
            for piece in pieces:
                wide = piece.astype(jnp.float32)
                square = wide * wide
                for lane in range(0, width, 128):
                    total = total + square[:, lane : lane + 128]
            mean_square = jnp.sum(total, axis=-1, keepdims=True) * (1.0 / (4 * width))
            scale = lax.rsqrt(mean_square + 1e-06)
            for piece, place in zip(pieces, places):
                scaled = piece.astype(jnp.float32) * scale * gain[:, pl.ds(place, width)]
                normed[at, pl.ds(place, width)] = scaled.astype(jnp.bfloat16)

        @pl.loop(0, half // tile)
        def _(step):
            start = pl.multiple_of(step * tile, tile)
            normalize(start, far_top, start)

        @pl.loop(0, half // tile)
        def _(step):
            start = pl.multiple_of(step * tile, tile)
            normalize(pl.multiple_of(half + start, tile), far_low, start)

        keyval = jnp.dot(normed[...], kv_weight[...], preferred_element_type=jnp.float32)
        ones = head_mean(head_dim, head_dim)
        keys = keyval[:, :head_dim]
        key = head_norm_rotary(keys, ones, k_gain[...], cosine[...], sine[...])[0]
        kv[:, :head_dim] = key.astype(jnp.bfloat16)
        kv[:, head_dim:] = keyval[:, head_dim:].astype(jnp.bfloat16)

    @pl.when(pl.program_id(0) > 0)
    def _():
        product = jnp.dot(normed[...], q_weight[...], preferred_element_type=jnp.float32)
        ones = head_mean(product.shape[1], head_dim)
        heads = head_norm_rotary(product, ones, q_gain[...], cosine[...], sine[...])
        for index, head in enumerate(heads):
            query[:, index * head_dim : (index + 1) * head_dim] = head.astype(jnp.bfloat16)


def project(me, pieces, gain, kv_weight, q_weight, k_gain, q_gain, cosine, sine, after):
    rows, width = pieces[0].shape
    depth, columns = q_weight.shape
    tile = 256
    whole = lambda array: pl.BlockSpec(array.shape, lambda n: (0, 0))
    tiles = lambda height: pl.BlockSpec((height, tile), lambda n: (0, jnp.maximum(n - 1, 0)))
    kv_shape = jax.ShapeDtypeStruct((rows, kv_weight.shape[1]), jnp.bfloat16)
    return pl.pallas_call(
        project_kernel,
        grid=(1 + columns // tile,),
        out_shape=(jax.ShapeDtypeStruct((rows, columns), jnp.bfloat16), kv_shape),
        in_specs=[pl.BlockSpec(memory_space=pltpu.SMEM)]
        + [whole(piece) for piece in pieces]
        + [whole(gain), whole(kv_weight), tiles(depth), whole(k_gain), whole(q_gain)]
        + [whole(cosine), whole(sine)]
        + [pl.BlockSpec(memory_space=pl.ANY)] * len(after),
        out_specs=[tiles(rows), whole(kv_shape)],
        scratch_shapes=[pltpu.VMEM((rows, depth), jnp.bfloat16)],
        compiler_params=pltpu.CompilerParams(vmem_limit_bytes=VMEM_BYTES),
        cost_estimate=TINY_COST,
        name="project",
    )(me, *pieces, gain, kv_weight, q_weight, k_gain, q_gain, cosine, sine, *after)


def forward_kernel(starts, after_count, *refs):
    count = len(starts)
    sources, outs, sems = refs[:count], refs[count + after_count : -1], refs[-1]
    copies = [
        pltpu.make_async_copy(source.at[pl.ds(start, out.shape[0]), :], out, sems.at[index])
        for index, (source, start, out) in enumerate(zip(sources, starts, outs))
    ]
    for copy in copies:
        copy.start()
    for copy in copies:
        copy.wait()


def take_rows(pieces, after):
    sources = [piece[0] for piece in pieces]
    return pl.pallas_call(
        functools.partial(forward_kernel, [piece[1] for piece in pieces], len(after)),
        out_shape=[
            jax.ShapeDtypeStruct((rows, source.shape[1]), source.dtype)
            for source, _, rows in pieces
        ],
        in_specs=[pl.BlockSpec(memory_space=pl.ANY)] * (len(sources) + len(after)),
        out_specs=[pl.BlockSpec(memory_space=pltpu.VMEM)] * len(pieces),
        scratch_shapes=[pltpu.SemaphoreType.DMA((len(pieces),))],
        compiler_params=pltpu.CompilerParams(vmem_limit_bytes=VMEM_BYTES),
        cost_estimate=TINY_COST,
        name="take_rows",
    )(*sources, *after)


def attention_kernel(
    page_base, chunk_count, session, start, prefix, query, prefix_kv, *refs
):
    kv_chunks = refs[:chunk_count]
    out, span = refs[-2:]
    step = pl.program_id(0)
    page = page_base + step
    head_dim = prefix_kv.shape[1] // 2
    page_size = query.shape[0]
    heads = query.shape[1] // head_dim
    rows = heads * page_size

    @pl.when(step == 0)
    def _():
        filled = 0
        for chunk in kv_chunks:
            span[pl.ds(filled, chunk.shape[0]), :] = chunk[...]
            filled += chunk.shape[0]
        if filled < span.shape[0]:
            span[filled:, :] = jnp.zeros((span.shape[0] - filled, span.shape[1]), span.dtype)

    split = rows // GROUPS
    grouped = jnp.concatenate(
        [query[:, h * head_dim : (h + 1) * head_dim] for h in range(heads)], axis=0
    )
    grouped = grouped.T
    groups = [grouped[:, g * split : (g + 1) * split] for g in range(GROUPS)]
    factor = LOG2E / float(head_dim) ** 0.5
    my_prefix = prefix[page]
    my_start = start[page]
    lanes = 128

    def key_index(count):
        return lax.broadcasted_iota(jnp.int32, (count, lanes), 0)

    def attend(span_rows):
        prefix_rows = prefix_kv.shape[0] // 4
        prefix_at = pl.multiple_of(session[page] * prefix_rows, prefix_rows)
        first = my_start * page_size
        span_at = pl.multiple_of(jnp.minimum(first, span.shape[0] - span_rows), page_size)
        token = lax.broadcasted_iota(jnp.int32, (span_rows, lanes), 1) & (page_size - 1)
        absolute = key_index(span_rows) + span_at
        parts = [
            (
                prefix_kv[pl.ds(prefix_at, prefix_rows), :],
                key_index(prefix_rows) < my_prefix * page_size,
            ),
            (
                span[pl.ds(span_at, span_rows), :],
                (absolute >= first) & (absolute <= page * page_size + token),
            ),
        ]
        biases = [
            jnp.concatenate([jnp.where(visible, 0.0, -jnp.inf)] * (split // lanes), axis=1)
            for _, visible in parts
        ]
        for g, group in enumerate(groups):
            scores = [
                jnp.dot(rows[:, :head_dim], group, preferred_element_type=jnp.float32) + bias
                for (rows, _), bias in zip(parts, biases)
            ]
            top = [jnp.max(score, axis=0, keepdims=True) for score in scores]
            top = jnp.maximum(top[0], top[1]) * factor
            weights = [jnp.exp2(score * factor - top) for score in scores]
            total = sum(jnp.sum(weight, axis=0, keepdims=True) for weight in weights)
            inverse = 1.0 / total
            mixed = sum(
                lax.dot_general(
                    rows[:, head_dim:],
                    (weight * inverse).astype(jnp.bfloat16),
                    (((0,), (0,)), ((), ())),
                    preferred_element_type=jnp.float32,
                )
                for (rows, _), weight in zip(parts, weights)
            )
            mixed = mixed.T.astype(jnp.bfloat16)
            for part in range(split // page_size):
                h = g * (split // page_size) + part
                out[:, h * head_dim : (h + 1) * head_dim] = mixed[
                    part * page_size : (part + 1) * page_size
                ]

    pages_seen = page - my_start + 1
    most = span.shape[0] // (2 * page_size)
    for low in range(0, most, SPAN_STEP):

        @pl.when((pages_seen > low) & (pages_seen <= low + SPAN_STEP))
        def _():
            attend((low + SPAN_STEP) * page_size)


def attention(
    page_base, layout, query, prefix_kv, kv_chunks, previous, row_count, page_size, after
):
    rows, columns = query.shape
    pages = rows // page_size
    whole = lambda shape: pl.BlockSpec(shape, lambda p, *_: (0, 0))
    operands = [query, prefix_kv, *kv_chunks]
    in_specs = [pl.BlockSpec((page_size, columns), lambda p, *_: (p, 0))]
    in_specs += [whole(operand.shape) for operand in operands[1:]]
    aliases = {}
    if previous is not None:
        aliases = {len(layout) + len(operands): 0}
        operands.append(previous)
        in_specs.append(pl.BlockSpec(memory_space=pl.ANY))
    operands += after
    in_specs += [pl.BlockSpec(memory_space=pl.ANY)] * len(after)
    return pl.pallas_call(
        functools.partial(attention_kernel, page_base, len(kv_chunks)),
        grid_spec=pltpu.PrefetchScalarGridSpec(
            num_scalar_prefetch=len(layout),
            grid=(pages,),
            in_specs=in_specs,
            out_specs=pl.BlockSpec((page_size, columns), lambda p, *_: (page_base + p, 0)),
            scratch_shapes=[pltpu.VMEM((row_count, prefix_kv.shape[1]), jnp.bfloat16)],
        ),
        out_shape=jax.ShapeDtypeStruct((row_count, columns), jnp.bfloat16),
        input_output_aliases=aliases,
        compiler_params=pltpu.CompilerParams(vmem_limit_bytes=VMEM_BYTES),
        cost_estimate=TINY_COST,
        name="attention",
    )(*layout, *operands)


def per_device(
    hidden_in,
    ln_gain,
    w_query,
    key_value_weight,
    q_gain,
    k_gain,
    key_value_cache,
    prefix_pages,
    page_holder,
    page_slot,
    span_pages,
    decode_target,
):
    replica = lax.axis_index("rep")
    me = lax.axis_index("tp").astype(jnp.int32)
    replicas = lax.axis_size("rep")
    parts = lax.axis_size("tp")
    up = [(i, (i + 1) % parts) for i in range(parts)]
    down = [(i, (i - 1) % parts) for i in range(parts)]
    head_dim = q_gain.shape[0]
    page_size = key_value_cache.shape[1]
    row_count = hidden_in.shape[0]
    page_count = row_count // page_size
    sessions = span_pages.shape[1]
    max_pages = page_holder.shape[2]
    capacity = sessions * max_pages // replicas
    push_slots = 2

    position_count = sessions * max_pages
    flat_holder = page_holder.reshape(replicas, position_count)
    flat_slot = page_slot.reshape(replicas, position_count)
    from_here = flat_holder == replica
    send_rank = jnp.cumsum(from_here.astype(jnp.int32), axis=1) - 1
    slot_range = jnp.arange(capacity, dtype=jnp.int32)
    matched = from_here[:, None, :] & (send_rank[:, None, :] == slot_range[None, :, None])
    local_ids = jnp.sum(jnp.where(matched, flat_slot[:, None, :], 0), -1)
    cache = key_value_cache.reshape(-1, page_size, 2 * head_dim)
    outgoing = jnp.take(cache, local_ids.reshape(-1), axis=0, mode="clip")
    outgoing = outgoing.reshape(replicas, capacity, page_size, 2 * head_dim)
    incoming = lax.all_to_all(outgoing, "rep", split_axis=0, concat_axis=0, tiled=True)
    incoming = incoming.reshape(replicas * capacity, page_size, 2 * head_dim)
    my_holder = lax.dynamic_index_in_dim(flat_holder, replica, 0, keepdims=False)
    position_index = jnp.arange(position_count, dtype=jnp.int32)
    same_earlier = (my_holder[:, None] == my_holder[None, :]) & (
        position_index[None, :] < position_index[:, None]
    )
    recv_rank = jnp.sum(same_earlier.astype(jnp.int32), axis=1)
    recv_ids = my_holder * capacity + recv_rank
    prefix_kv = jnp.take(incoming, recv_ids, axis=0, mode="clip")
    prefix_kv = prefix_kv.reshape(position_count * page_size, 2 * head_dim)

    my_span = lax.dynamic_index_in_dim(span_pages, replica, 0, keepdims=False)
    my_prefix = lax.dynamic_index_in_dim(prefix_pages, replica, 0, keepdims=False)
    layout = page_layout(my_span, my_prefix, page_count)
    session_of, start_of, prefix_of = layout
    page_index = jnp.arange(page_count, dtype=jnp.int32)
    page_first = (prefix_of + page_index - start_of) * page_size
    positions = (page_first[:, None] + jnp.arange(page_size, dtype=jnp.int32)[None, :]).reshape(-1)
    cosine, sine = rotary_tables(positions, head_dim)

    targets = decode_target[..., 0]
    my_targets = lax.dynamic_index_in_dim(targets, replica, 0, keepdims=True)
    my_ranks = target_ranks(my_targets)[0]
    wanted = jnp.arange(replicas * push_slots, dtype=jnp.int32)
    chosen = (my_targets[0] * push_slots + my_ranks)[None, :] == wanted[:, None]
    push_ids = jnp.sum(jnp.where(chosen, page_index[None, :], 0), -1)
    push_valid = jnp.any(chosen, axis=-1).astype(jnp.int32)

    gain = ln_gain.reshape(1, -1)
    kv_weight = key_value_weight.reshape(key_value_weight.shape[0], -1)
    q_gain, k_gain = q_gain.reshape(1, -1), k_gain.reshape(1, -1)
    count = len(CHUNK_PAGES)
    sizes = [pages * page_size for pages in CHUNK_PAGES]
    offsets = [sum(sizes[:index]) for index in range(count)]
    own, near, far = {}, {}, {}

    def send_near(index, rows):
        own[index] = rows
        near[index] = lax.ppermute(rows, "tp", up), lax.ppermute(rows, "tp", down)

    def send_far(index, after):
        half = sizes[index] // 2
        left, right = near[index]
        pieces = [(left, 0, half), (right, half, half)]
        following = index + 1 if index else count
        if following < count:
            pieces.append((hidden_in, offsets[following], sizes[following]))
        copies = take_rows(pieces, after)
        far[index] = lax.ppermute(copies[0], "tp", up), lax.ppermute(copies[1], "tp", down)
        if following < count:
            send_near(following, copies[2])
        return copies[0]

    for index in range(2):
        send_near(index, hidden_in[offsets[index] : offsets[index] + sizes[index]])
    send_far(0, [])
    tables = [
        (cosine[offset : offset + size], sine[offset : offset + size])
        for offset, size in zip(offsets, sizes)
    ]
    early = [table for pair in tables for table in pair]
    last = [send_far(1, [*far[0], *early, push_ids, push_valid, prefix_kv])]
    kv_chunks, queries, attn_out = [], [], None

    def run_project(index, last):
        chunk = (own[index], *near[index], *far[index])
        weights = kv_weight, w_query, k_gain, q_gain
        query, kv = project(me[None], chunk, gain, *weights, *tables[index], last)
        queries.append(query)
        kv_chunks.append(kv)
        return [kv]

    def run_attention(index, previous, last):
        return attention(
            offsets[index] // page_size,
            layout,
            queries[index],
            prefix_kv,
            kv_chunks[: index + 1],
            previous,
            row_count,
            page_size,
            last,
        )

    for index in range(count - 1):
        last = run_project(index, last)
        if index < count - 2:
            attn_out = run_attention(index, attn_out, last)
            last = [send_far(index + 2, [attn_out, *far[index + 1]])]
    last = run_project(count - 1, last)
    fresh = jnp.concatenate(kv_chunks, 0).reshape(page_count, page_size, 2 * head_dim)
    pushing = jnp.take(fresh, push_ids, axis=0, mode="clip")
    pushing = jnp.where(push_valid[:, None, None] > 0, pushing, jnp.zeros_like(pushing))
    pushing = pushing.reshape(replicas, push_slots, page_size, 2 * head_dim)
    pushed = lax.all_to_all(pushing, "rep", split_axis=0, concat_axis=0, tiled=True)
    attn_out = run_attention(count - 2, attn_out, [pushing])
    attn_out = run_attention(count - 1, attn_out, [])
    pushed = pushed.reshape(replicas * push_slots, page_size, 1, 2 * head_dim)
    return (attn_out, pushed)


def solution(mesh):
    placed = (
        P("rep", "tp"),
        P(),
        P(None, "tp"),
        P(None, "tp", None),
        P(),
        P(),
        P("rep", None, "tp", None),
        P(),
        P(),
        P(),
        P(),
        P(),
    )
    return jax.shard_map(
        per_device,
        mesh=mesh,
        in_specs=placed,
        out_specs=(P("rep", "tp"), P("rep", None, "tp", None)),
        check_vma=False,
    )
```

```python
import functools

import jax
import jax.numpy as jnp
from jax import lax
from jax.experimental import pallas as pl
from jax.experimental.pallas import tpu as pltpu
from jax.sharding import PartitionSpec as P

CHUNK_PAGES = (8, 8, 8)
GROUPS = 1
NORM_ROWS = 64
SPAN_STEP = 4
VMEM_BYTES = 56 * 1024 * 1024
TINY_COST = pl.CostEstimate(flops=1, bytes_accessed=1, transcendentals=0)
LOG2E = 1.4426950408889634


def rotary_tables(positions, head_dim):
    half_dim = head_dim // 2
    exponent = jnp.arange(half_dim, dtype=jnp.float32) * (2.0 / head_dim)
    inverse = jnp.power(jnp.float32(1000000.0), -exponent)
    angles = positions.astype(jnp.float32)[:, None] * inverse[None, :]
    cosine, sine = jnp.cos(angles), jnp.sin(angles)
    return jnp.concatenate([cosine, cosine], -1), jnp.concatenate([-sine, sine], -1)


def page_layout(span_counts, prefix_counts, page_count):
    ends = jnp.cumsum(span_counts, axis=0)
    starts = ends - span_counts
    page_index = jnp.arange(page_count, dtype=jnp.int32)
    session_of = jnp.sum((page_index[:, None] >= ends[None, :]).astype(jnp.int32), -1)
    onehot = session_of[:, None] == jnp.arange(span_counts.shape[0], dtype=jnp.int32)
    start_of = jnp.sum(jnp.where(onehot, starts[None, :], 0), -1)
    prefix_of = jnp.sum(jnp.where(onehot, prefix_counts[None, :], 0), -1)
    return session_of, start_of, prefix_of


def target_ranks(targets):
    count = targets.shape[1]
    order = jnp.arange(count, dtype=jnp.int32)
    earlier = (targets[:, :, None] == targets[:, None, :]) & (
        order[None, None, :] < order[None, :, None]
    )
    return jnp.sum(earlier.astype(jnp.int32), -1)


def head_norm_rotary(values, ones, gain, cosine, sine):
    square = values * values
    high = square.astype(jnp.bfloat16)
    low = (square - high.astype(jnp.float32)).astype(jnp.bfloat16)
    mean_square = jnp.dot(high, ones, preferred_element_type=jnp.float32)
    mean_square = mean_square + jnp.dot(low, ones, preferred_element_type=jnp.float32)
    scaled = values * lax.rsqrt(mean_square + 1e-06)
    head_dim = gain.shape[1]
    heads = []
    for start in range(0, values.shape[1], head_dim):
        head = scaled[:, start : start + head_dim] * gain
        heads.append(head * cosine + pltpu.roll(head, head_dim // 2, axis=1) * sine)
    return heads


def head_mean(columns, head_dim):
    column = lax.broadcasted_iota(jnp.int32, (columns, columns), 1)
    row = lax.broadcasted_iota(jnp.int32, (columns, columns), 0)
    same = lax.div(row, head_dim) == lax.div(column, head_dim)
    return jnp.where(same, 1.0 / head_dim, 0.0).astype(jnp.bfloat16)


def project_kernel(
    me_ref,
    own,
    left,
    right,
    far_top,
    far_low,
    gain,
    kv_weight,
    q_weight,
    k_gain,
    q_gain,
    cosine,
    sine,
    *refs,
):
    query, kv, normed = refs[-3:]
    rows, width = own.shape
    half = rows // 2
    head_dim = k_gain.shape[1]

    @pl.when(pl.program_id(0) == 0)
    def _():
        me = me_ref[0]
        tile = NORM_ROWS
        places = [pl.multiple_of(lax.rem(me + shift, 4) * width, 128) for shift in (0, 3, 1, 2)]

        def normalize(start, far, far_start):
            at = pl.ds(start, tile)
            pieces = [own[at, :], left[at, :], right[at, :], far[pl.ds(far_start, tile), :]]
            total = jnp.zeros((tile, 128), jnp.float32)
            for piece in pieces:
                wide = piece.astype(jnp.float32)
                square = wide * wide
                for lane in range(0, width, 128):
                    total = total + square[:, lane : lane + 128]
            mean_square = jnp.sum(total, axis=-1, keepdims=True) * (1.0 / (4 * width))
            scale = lax.rsqrt(mean_square + 1e-06)
            for piece, place in zip(pieces, places):
                scaled = piece.astype(jnp.float32) * scale * gain[:, pl.ds(place, width)]
                normed[at, pl.ds(place, width)] = scaled.astype(jnp.bfloat16)

        @pl.loop(0, half // tile)
        def _(step):
            start = pl.multiple_of(step * tile, tile)
            normalize(start, far_top, start)

        @pl.loop(0, half // tile)
        def _(step):
            start = pl.multiple_of(step * tile, tile)
            normalize(pl.multiple_of(half + start, tile), far_low, start)

        keyval = jnp.dot(normed[...], kv_weight[...], preferred_element_type=jnp.float32)
        ones = head_mean(head_dim, head_dim)
        keys = keyval[:, :head_dim]
        key = head_norm_rotary(keys, ones, k_gain[...], cosine[...], sine[...])[0]
        kv[:, :head_dim] = key.astype(jnp.bfloat16)
        kv[:, head_dim:] = keyval[:, head_dim:].astype(jnp.bfloat16)

    @pl.when(pl.program_id(0) > 0)
    def _():
        product = jnp.dot(normed[...], q_weight[...], preferred_element_type=jnp.float32)
        ones = head_mean(product.shape[1], head_dim)
        heads = head_norm_rotary(product, ones, q_gain[...], cosine[...], sine[...])
        for index, head in enumerate(heads):
            query[:, index * head_dim : (index + 1) * head_dim] = head.astype(jnp.bfloat16)


def project(me, pieces, gain, kv_weight, q_weight, k_gain, q_gain, cosine, sine, after):
    rows, width = pieces[0].shape
    depth, columns = q_weight.shape
    tile = 256
    whole = lambda array: pl.BlockSpec(array.shape, lambda n: (0, 0))
    tiles = lambda height: pl.BlockSpec((height, tile), lambda n: (0, jnp.maximum(n - 1, 0)))
    kv_shape = jax.ShapeDtypeStruct((rows, kv_weight.shape[1]), jnp.bfloat16)
    return pl.pallas_call(
        project_kernel,
        grid=(1 + columns // tile,),
        out_shape=(jax.ShapeDtypeStruct((rows, columns), jnp.bfloat16), kv_shape),
        in_specs=[pl.BlockSpec(memory_space=pltpu.SMEM)]
        + [whole(piece) for piece in pieces]
        + [whole(gain), whole(kv_weight), tiles(depth), whole(k_gain), whole(q_gain)]
        + [whole(cosine), whole(sine)]
        + [pl.BlockSpec(memory_space=pl.ANY)] * len(after),
        out_specs=[tiles(rows), whole(kv_shape)],
        scratch_shapes=[pltpu.VMEM((rows, depth), jnp.bfloat16)],
        compiler_params=pltpu.CompilerParams(vmem_limit_bytes=VMEM_BYTES),
        cost_estimate=TINY_COST,
        name="project",
    )(me, *pieces, gain, kv_weight, q_weight, k_gain, q_gain, cosine, sine, *after)


def forward_kernel(starts, after_count, *refs):
    count = len(starts)
    sources, outs, sems = refs[:count], refs[count + after_count : -1], refs[-1]
    copies = [
        pltpu.make_async_copy(source.at[pl.ds(start, out.shape[0]), :], out, sems.at[index])
        for index, (source, start, out) in enumerate(zip(sources, starts, outs))
    ]
    for copy in copies:
        copy.start()
    for copy in copies:
        copy.wait()


def take_rows(pieces, after):
    sources = [piece[0] for piece in pieces]
    return pl.pallas_call(
        functools.partial(forward_kernel, [piece[1] for piece in pieces], len(after)),
        out_shape=[
            jax.ShapeDtypeStruct((rows, source.shape[1]), source.dtype)
            for source, _, rows in pieces
        ],
        in_specs=[pl.BlockSpec(memory_space=pl.ANY)] * (len(sources) + len(after)),
        out_specs=[pl.BlockSpec(memory_space=pltpu.VMEM)] * len(pieces),
        scratch_shapes=[pltpu.SemaphoreType.DMA((len(pieces),))],
        compiler_params=pltpu.CompilerParams(vmem_limit_bytes=VMEM_BYTES),
        cost_estimate=TINY_COST,
        name="take_rows",
    )(*sources, *after)


def attention_kernel(
    page_base, chunk_count, session, start, prefix, query, prefix_kv, *refs
):
    kv_chunks = refs[:chunk_count]
    out, span = refs[-2:]
    step = pl.program_id(0)
    page = page_base + step
    head_dim = prefix_kv.shape[1] // 2
    page_size = query.shape[0]
    heads = query.shape[1] // head_dim
    rows = heads * page_size

    @pl.when(step == 0)
    def _():
        filled = 0
        for chunk in kv_chunks:
            span[pl.ds(filled, chunk.shape[0]), :] = chunk[...]
            filled += chunk.shape[0]
        if filled < span.shape[0]:
            span[filled:, :] = jnp.zeros((span.shape[0] - filled, span.shape[1]), span.dtype)

    split = rows // GROUPS
    grouped = jnp.concatenate(
        [query[:, h * head_dim : (h + 1) * head_dim] for h in range(heads)], axis=0
    )
    grouped = grouped.T
    groups = [grouped[:, g * split : (g + 1) * split] for g in range(GROUPS)]
    factor = LOG2E / float(head_dim) ** 0.5
    my_prefix = prefix[page]
    my_start = start[page]
    lanes = 128

    def key_index(count):
        return lax.broadcasted_iota(jnp.int32, (count, lanes), 0)

    def attend(span_rows):
        prefix_rows = prefix_kv.shape[0] // 4
        prefix_at = pl.multiple_of(session[page] * prefix_rows, prefix_rows)
        first = my_start * page_size
        span_at = pl.multiple_of(jnp.minimum(first, span.shape[0] - span_rows), page_size)
        token = lax.broadcasted_iota(jnp.int32, (span_rows, lanes), 1) & (page_size - 1)
        absolute = key_index(span_rows) + span_at
        parts = [
            (
                prefix_kv[pl.ds(prefix_at, prefix_rows), :],
                key_index(prefix_rows) < my_prefix * page_size,
            ),
            (
                span[pl.ds(span_at, span_rows), :],
                (absolute >= first) & (absolute <= page * page_size + token),
            ),
        ]
        biases = [
            jnp.concatenate([jnp.where(visible, 0.0, -jnp.inf)] * (split // lanes), axis=1)
            for _, visible in parts
        ]
        for g, group in enumerate(groups):
            scores = [
                jnp.dot(rows[:, :head_dim], group, preferred_element_type=jnp.float32) + bias
                for (rows, _), bias in zip(parts, biases)
            ]
            top = [jnp.max(score, axis=0, keepdims=True) for score in scores]
            top = jnp.maximum(top[0], top[1]) * factor
            weights = [jnp.exp2(score * factor - top) for score in scores]
            total = sum(jnp.sum(weight, axis=0, keepdims=True) for weight in weights)
            inverse = 1.0 / total
            mixed = sum(
                lax.dot_general(
                    rows[:, head_dim:],
                    (weight * inverse).astype(jnp.bfloat16),
                    (((0,), (0,)), ((), ())),
                    preferred_element_type=jnp.float32,
                )
                for (rows, _), weight in zip(parts, weights)
            )
            mixed = mixed.T.astype(jnp.bfloat16)
            for part in range(split // page_size):
                h = g * (split // page_size) + part
                out[:, h * head_dim : (h + 1) * head_dim] = mixed[
                    part * page_size : (part + 1) * page_size
                ]

    pages_seen = page - my_start + 1
    most = span.shape[0] // (2 * page_size)
    for low in range(0, most, SPAN_STEP):

        @pl.when((pages_seen > low) & (pages_seen <= low + SPAN_STEP))
        def _():
            attend((low + SPAN_STEP) * page_size)


def attention(
    page_base, layout, query, prefix_kv, kv_chunks, previous, row_count, page_size, after
):
    rows, columns = query.shape
    pages = rows // page_size
    whole = lambda shape: pl.BlockSpec(shape, lambda p, *_: (0, 0))
    operands = [query, prefix_kv, *kv_chunks]
    in_specs = [pl.BlockSpec((page_size, columns), lambda p, *_: (p, 0))]
    in_specs += [whole(operand.shape) for operand in operands[1:]]
    aliases = {}
    if previous is not None:
        aliases = {len(layout) + len(operands): 0}
        operands.append(previous)
        in_specs.append(pl.BlockSpec(memory_space=pl.ANY))
    operands += after
    in_specs += [pl.BlockSpec(memory_space=pl.ANY)] * len(after)
    return pl.pallas_call(
        functools.partial(attention_kernel, page_base, len(kv_chunks)),
        grid_spec=pltpu.PrefetchScalarGridSpec(
            num_scalar_prefetch=len(layout),
            grid=(pages,),
            in_specs=in_specs,
            out_specs=pl.BlockSpec((page_size, columns), lambda p, *_: (page_base + p, 0)),
            scratch_shapes=[pltpu.VMEM((row_count, prefix_kv.shape[1]), jnp.bfloat16)],
        ),
        out_shape=jax.ShapeDtypeStruct((row_count, columns), jnp.bfloat16),
        input_output_aliases=aliases,
        compiler_params=pltpu.CompilerParams(vmem_limit_bytes=VMEM_BYTES),
        cost_estimate=TINY_COST,
        name="attention",
    )(*layout, *operands)


def per_device(
    hidden_in,
    ln_gain,
    w_query,
    key_value_weight,
    q_gain,
    k_gain,
    key_value_cache,
    prefix_pages,
    page_holder,
    page_slot,
    span_pages,
    decode_target,
):
    replica = lax.axis_index("rep")
    me = lax.axis_index("tp").astype(jnp.int32)
    replicas = lax.axis_size("rep")
    parts = lax.axis_size("tp")
    up = [(i, (i + 1) % parts) for i in range(parts)]
    down = [(i, (i - 1) % parts) for i in range(parts)]
    head_dim = q_gain.shape[0]
    page_size = key_value_cache.shape[1]
    row_count = hidden_in.shape[0]
    page_count = row_count // page_size
    sessions = span_pages.shape[1]
    max_pages = page_holder.shape[2]
    capacity = sessions * max_pages // replicas
    push_slots = 2

    position_count = sessions * max_pages
    flat_holder = page_holder.reshape(replicas, position_count)
    flat_slot = page_slot.reshape(replicas, position_count)
    from_here = flat_holder == replica
    send_rank = jnp.cumsum(from_here.astype(jnp.int32), axis=1) - 1
    slot_range = jnp.arange(capacity, dtype=jnp.int32)
    matched = from_here[:, None, :] & (send_rank[:, None, :] == slot_range[None, :, None])
    local_ids = jnp.sum(jnp.where(matched, flat_slot[:, None, :], 0), -1)
    cache = key_value_cache.reshape(-1, page_size, 2 * head_dim)
    outgoing = jnp.take(cache, local_ids.reshape(-1), axis=0, mode="clip")
    outgoing = outgoing.reshape(replicas, capacity, page_size, 2 * head_dim)
    incoming = lax.all_to_all(outgoing, "rep", split_axis=0, concat_axis=0, tiled=True)
    incoming = incoming.reshape(replicas * capacity, page_size, 2 * head_dim)
    my_holder = lax.dynamic_index_in_dim(flat_holder, replica, 0, keepdims=False)
    position_index = jnp.arange(position_count, dtype=jnp.int32)
    same_earlier = (my_holder[:, None] == my_holder[None, :]) & (
        position_index[None, :] < position_index[:, None]
    )
    recv_rank = jnp.sum(same_earlier.astype(jnp.int32), axis=1)
    recv_ids = my_holder * capacity + recv_rank
    prefix_kv = jnp.take(incoming, recv_ids, axis=0, mode="clip")
    prefix_kv = prefix_kv.reshape(position_count * page_size, 2 * head_dim)

    my_span = lax.dynamic_index_in_dim(span_pages, replica, 0, keepdims=False)
    my_prefix = lax.dynamic_index_in_dim(prefix_pages, replica, 0, keepdims=False)
    layout = page_layout(my_span, my_prefix, page_count)
    session_of, start_of, prefix_of = layout
    page_index = jnp.arange(page_count, dtype=jnp.int32)
    page_first = (prefix_of + page_index - start_of) * page_size
    positions = (page_first[:, None] + jnp.arange(page_size, dtype=jnp.int32)[None, :]).reshape(-1)
    cosine, sine = rotary_tables(positions, head_dim)

    targets = decode_target[..., 0]
    my_targets = lax.dynamic_index_in_dim(targets, replica, 0, keepdims=True)
    my_ranks = target_ranks(my_targets)[0]
    wanted = jnp.arange(replicas * push_slots, dtype=jnp.int32)
    chosen = (my_targets[0] * push_slots + my_ranks)[None, :] == wanted[:, None]
    push_ids = jnp.sum(jnp.where(chosen, page_index[None, :], 0), -1)
    push_valid = jnp.any(chosen, axis=-1).astype(jnp.int32)

    gain = ln_gain.reshape(1, -1)
    kv_weight = key_value_weight.reshape(key_value_weight.shape[0], -1)
    q_gain, k_gain = q_gain.reshape(1, -1), k_gain.reshape(1, -1)
    count = len(CHUNK_PAGES)
    sizes = [pages * page_size for pages in CHUNK_PAGES]
    offsets = [sum(sizes[:index]) for index in range(count)]
    own, near, far = {}, {}, {}

    def send_near(index, rows):
        own[index] = rows
        near[index] = lax.ppermute(rows, "tp", up), lax.ppermute(rows, "tp", down)

    def send_far(index, after):
        half = sizes[index] // 2
        left, right = near[index]
        pieces = [(left, 0, half), (right, half, half)]
        following = index + 1 if index else count
        if following < count:
            pieces.append((hidden_in, offsets[following], sizes[following]))
        copies = take_rows(pieces, after)
        far[index] = lax.ppermute(copies[0], "tp", up), lax.ppermute(copies[1], "tp", down)
        if following < count:
            send_near(following, copies[2])
        return copies[0]

    for index in range(2):
        send_near(index, hidden_in[offsets[index] : offsets[index] + sizes[index]])
    send_far(0, [])
    tables = [
        (cosine[offset : offset + size], sine[offset : offset + size])
        for offset, size in zip(offsets, sizes)
    ]
    early = [table for pair in tables for table in pair]
    last = [send_far(1, [*far[0], *early, push_ids, push_valid, prefix_kv])]
    kv_chunks, queries, attn_out = [], [], None

    def run_project(index, last):
        chunk = (own[index], *near[index], *far[index])
        weights = kv_weight, w_query, k_gain, q_gain
        query, kv = project(me[None], chunk, gain, *weights, *tables[index], last)
        queries.append(query)
        kv_chunks.append(kv)
        return [kv]

    def run_attention(index, previous, last):
        return attention(
            offsets[index] // page_size,
            layout,
            queries[index],
            prefix_kv,
            kv_chunks[: index + 1],
            previous,
            row_count,
            page_size,
            last,
        )

    for index in range(count - 1):
        last = run_project(index, last)
        if index < count - 2:
            attn_out = run_attention(index, attn_out, last)
            last = [send_far(index + 2, [attn_out, *far[index + 1]])]
    last = run_project(count - 1, last)
    fresh = jnp.concatenate(kv_chunks, 0).reshape(page_count, page_size, 2 * head_dim)
    pushing = jnp.take(fresh, push_ids, axis=0, mode="clip")
    pushing = jnp.where(push_valid[:, None, None] > 0, pushing, jnp.zeros_like(pushing))
    pushing = pushing.reshape(replicas, push_slots, page_size, 2 * head_dim)
    pushed = lax.all_to_all(pushing, "rep", split_axis=0, concat_axis=0, tiled=True)
    attn_out = run_attention(count - 2, attn_out, [pushing])
    attn_out = run_attention(count - 1, attn_out, [])
    pushed = pushed.reshape(replicas * push_slots, page_size, 1, 2 * head_dim)
    return (attn_out, pushed)


def solution(mesh):
    placed = (
        P("rep", "tp"),
        P(),
        P(None, "tp"),
        P(None, "tp", None),
        P(),
        P(),
        P("rep", None, "tp", None),
        P(),
        P(),
        P(),
        P(),
        P(),
    )
    return jax.shard_map(
        per_device,
        mesh=mesh,
        in_specs=placed,
        out_specs=(P("rep", "tp"), P("rep", None, "tp", None)),
        check_vma=False,
    )
```
